32 devices in a mesh: group: 2 (over x), hst: 16 (over z, y, core).
Axes of the slice: x: 2, y: 2, z: 4, core: 2. Of those that a mesh axis runs over, the one named last changes fastest.
Arguments:
- tokens: bfloat16 [1024, 4096], P(('group', 'hst')), parts along dimension 0, may hold values from -6 to 6
- routes: int32 [1024, 8], P(('group', 'hst')), parts along dimension 0, may hold values from 0 to 15, all different within a row; in each aligned block of 32 rows (0 to 31, 32 to 63, ...) at most 32 rows name the same one
- gate_code: int32 [1024, 8], P(('group', 'hst')), parts along dimension 0, may hold values from 1 to 65535
- w_gate: bfloat16 [16, 4096, 768], P('hst'), may hold values from -0.09375 to 0.09375
- w_up: bfloat16 [16, 4096, 768], P('hst'), may hold values from -0.09375 to 0.09375
- w_down: bfloat16 [16, 768, 4096], P('hst'), may hold values from -0.21875 to 0.21875
Outputs:
- moe_out: bfloat16 [1024, 4096], P(('group', 'hst')), parts along dimension 0
The draws below stay inside these ranges and needn't reach their ends.
There are 2 independent parts, one for each index of `group`. The reference program is written for one: setup_inputs(seed, part) draws one part's arguments, and reference() takes and returns one part's arrays. A program takes and returns all parts, laid end to end along the dimension named above; an argument that names none is the same for every part. Nothing has to cross between parts.
Inputs may be any that keep to these rules, and one draw needn't show every extreme that they name: `routes`: each row names 8 different experts. Among the rows of one index of hst no expert is named more than 32 times, a bound that some block reaches there in every draw; every expert is named somewhere.
All inputs are finite; a program needn't handle non-finite values.
Results may differ from the reference program's by a relative error of at most 0.008.
Values may be sent and summed in bfloat16 or wider, within the bound.
A program may use at most 128 MiB of HBM per device.

```python
import math
import jax
import jax.numpy as jnp
import numpy as np
from jax import lax

D = 4096
FF = 768
TOPK = 8
TOK_DEV = 32
EXPERTS = 16
CAP = 32
TOKENS = 512
N_HST = 16


def set_ends(values, rng, low, high):
    spot = [jax.random.randint(jax.random.fold_in(rng, axis), (), 0, length) for axis, length in enumerate(values.shape)]
    widest = values.shape.index(max(values.shape))
    next_to = spot[:widest] + [(spot[widest] + 1) % values.shape[widest]] + spot[widest + 1:]
    return values.at[tuple(spot)].set(low).at[tuple(next_to)].set(high)


def steps_of(stream_key, dims, shards, smallest, high):
    gain, own = 1.0, jax.random.fold_in(stream_key, 6)
    for axis_at, parts in shards:
        draws = jnp.exp(jax.random.uniform(jax.random.fold_in(own, axis_at), (parts,), jnp.float32, smallest / len(shards), high / len(shards)))
        gain = gain * jnp.repeat(draws, dims[axis_at] // parts).reshape([-1 if axis == axis_at else 1 for axis in range(len(dims))])
    return gain


def deal_out(own_key, own, number, rows, number_of, top, limit, slope):
    order = jax.random.permutation(own_key, number_of)
    crowded, usual = load_shares(number_of, rows * top, limit, slope, True), load_shares(number_of, rows * top, limit, slope, False)
    places = jnp.arange(number_of)

    def named(tallies, rotation):
        used = int((tallies > 0).sum())
        fixed = max(1, used // 4)
        moved = fixed + (places - fixed + rotation * (used - fixed)) % max(1, number_of - fixed)
        return jnp.zeros((number_of,), jnp.int32).at[order[jnp.where(places < fixed, places, moved)]].set(jnp.asarray(tallies, jnp.int32))

    tallies = jnp.where(number % 4 == 0, named(crowded, number // 4), named(usual, number - number // 4 - 1))
    mixed = jax.random.permutation(jax.random.fold_in(own, 3), number_of)
    donor, taker = mixed[0:number_of // 2 * 2:2], mixed[1:number_of // 2 * 2:2]
    room = jnp.minimum(tallies[donor] - 1, limit - tallies[taker]) // 2
    room = jnp.where((donor == order[0]) | (taker == order[0]) | (tallies[taker] == 0), 0, jnp.maximum(room, 0))
    moved = jax.random.randint(jax.random.fold_in(own, 4), (number_of // 2,), 0, 1 << 20) % (room + 1)
    tallies = tallies.at[donor].add(-moved).at[taker].add(moved)
    members = jnp.searchsorted(jnp.cumsum(tallies), jnp.arange(rows * top), side="right").astype(jnp.int32)
    grid = members.reshape(top, rows).T
    grid = grid[jax.random.permutation(jax.random.fold_in(own, 1), rows)]
    rotation = jax.random.randint(jax.random.fold_in(own, 2), (rows, 1), 0, top)
    return jnp.take_along_axis(grid, (jnp.arange(top)[None, :] + rotation) % top, axis=1)


def load_shares(count, total, limit, skew, full):
    portions = [(1 << 20) // math.isqrt(grade ** skew) + 1 for grade in range(1, count + 1)]
    largest = limit if full else min(limit, max(-(-total // count), total * portions[0] // sum(portions)))
    least = 1 if total - largest >= count - 1 else 0
    holding, rest = [largest] + [least] * (count - 1), total - largest - least * (count - 1)
    while rest > 0:
        movable = [i for i in range(1, count) if holding[i] < largest] or [i for i in range(1, count) if holding[i] < limit]
        whole, budget = sum([portions[i] for i in movable]), rest
        for i in movable:
            addition = min(limit - holding[i], max(1, budget * portions[i] // whole), rest)
            holding[i] = holding[i] + addition
            rest = rest - addition
    return np.array(holding)


def noise(stream_key, shape, spread, limit, cuts=(), held_as=jnp.bfloat16):
    level = steps_of(stream_key, shape, cuts, -0.22, 0.18) if cuts else 1.0
    result = jax.random.normal(stream_key, shape, jnp.float32) * spread * level
    return jnp.minimum(jnp.maximum(result, -limit), limit).astype(held_as)


def setup_inputs(seed: int = 0, part: int = 0) -> dict:
    keys = jax.random.split(jax.random.key(seed), 7)
    part_splits = jax.random.split(jax.random.fold_in(keys[6], part), 7)
    tokens = noise(part_splits[0], (TOKENS, D), 1.0, 6.0, ((0, 16),))
    routes_keys = jax.random.split(jax.random.fold_in(part_splits[1], 1), TOKENS // TOK_DEV)
    routes_turns = jax.random.permutation(jax.random.fold_in(part_splits[1], 3), TOKENS // TOK_DEV)
    routes = jax.vmap(lambda own, number: deal_out(jax.random.fold_in(part_splits[1], 2), own, number, TOK_DEV, EXPERTS, TOPK, CAP, 2))(routes_keys, routes_turns).reshape((TOKENS, TOPK))
    gate_code = set_ends(jax.random.randint(part_splits[2], (TOKENS, TOPK), 1, 65536), jax.random.fold_in(part_splits[2], 1), 1, 65535).astype(jnp.int32)
    w_gate = noise(keys[3], (EXPERTS, D, FF), D ** -0.5, 0.09375, ((0, 16),))
    w_up = noise(keys[4], (EXPERTS, D, FF), D ** -0.5, 0.09375, ((0, 16),))
    w_down = noise(keys[5], (EXPERTS, FF, D), FF ** -0.5, 0.21875, ((0, 16),))
    return dict(tokens=tokens, routes=routes, gate_code=gate_code, w_gate=w_gate, w_up=w_up, w_down=w_down)


def expert_ffn(block_rows, gate_mat, up_mat, down_mat):
    gate_h = jnp.dot(block_rows, gate_mat, preferred_element_type=jnp.float32)
    up_h = jnp.dot(block_rows, up_mat, preferred_element_type=jnp.float32)
    hidden = (jax.nn.silu(gate_h) * up_h).astype(jnp.bfloat16)
    return jnp.dot(hidden, down_mat, preferred_element_type=jnp.float32).astype(jnp.bfloat16)


def reference(tokens, routes, gate_code, w_gate, w_up, w_down):
    top_count = routes.shape[1]
    grouped = routes.reshape(N_HST, TOK_DEV * top_count)
    onehot = (grouped[:, :, None] == jnp.arange(EXPERTS, dtype=jnp.int32)[None, None, :]).astype(jnp.int32)
    earlier = jnp.cumsum(onehot, axis=1) - onehot
    slot_index = jnp.sum(earlier * onehot, axis=2).astype(jnp.int32)
    source = jnp.arange(N_HST, dtype=jnp.int32)[:, None]
    target = (grouped * (N_HST * CAP) + source * CAP + slot_index).reshape(-1).astype(jnp.int32)
    token_ids = jnp.repeat(jnp.arange(TOKENS, dtype=jnp.int32), top_count)
    slot_table = jnp.zeros((EXPERTS * N_HST * CAP,), jnp.int32).at[target].set(token_ids + 1)
    slot_table = slot_table.reshape(EXPERTS, N_HST * CAP)

    def run_expert(expert):
        entry = slot_table[expert]
        block_rows = tokens[jnp.maximum(entry - 1, 0)] * (entry > 0)[:, None].astype(tokens.dtype)
        return expert_ffn(block_rows, w_gate[expert], w_up[expert], w_down[expert])

    expert_out = lax.map(run_expert, jnp.arange(EXPERTS, dtype=jnp.int32))
    flat_out = expert_out.reshape(-1, D)
    picked = flat_out[target].reshape(TOKENS, top_count, D)
    codes = gate_code.astype(jnp.float32)
    gate_weights = codes / jnp.sum(codes, axis=1, keepdims=True)
    mixed = jnp.einsum("tk,tkd->td", gate_weights, picked.astype(jnp.float32))
    return mixed.astype(jnp.bfloat16)
```

```python
import jax
import jax.numpy as jnp
from jax import lax
from jax.sharding import PartitionSpec as P


def local(tokens, routes, gate_code, w_gate, w_up, w_down):
    n = lax.axis_size("hst")
    experts = n * w_gate.shape[0]
    me = lax.axis_index("hst")
    codes = gate_code.astype(jnp.float32)
    hits = (routes[:, :, None] == jnp.arange(experts, dtype=jnp.int32)[None, None, :]).astype(jnp.float32)
    weights = jnp.sum(hits * codes[:, :, None], axis=1) / jnp.sum(codes, axis=1, keepdims=True)
    all_weights = lax.all_gather(weights, "hst", axis=0, tiled=True)
    mine = lax.dynamic_slice_in_dim(all_weights, me, 1, axis=1)
    rows = lax.all_gather(tokens, "hst", axis=0, tiled=True)
    gate_h = jnp.dot(rows, w_gate[0], preferred_element_type=jnp.float32)
    up_h = jnp.dot(rows, w_up[0], preferred_element_type=jnp.float32)
    hidden = (jax.nn.silu(gate_h) * up_h).astype(jnp.bfloat16)
    out = jnp.dot(hidden, w_down[0], preferred_element_type=jnp.float32)
    part = (out * mine).astype(jnp.bfloat16)
    return lax.psum_scatter(part, "hst", scatter_dimension=0, tiled=True)


def solution(mesh):
    rows = P(("group", "hst"), None)
    whole = P("hst", None, None)
    return jax.shard_map(local, mesh=mesh, in_specs=(rows, rows, rows, whole, whole, whole), out_specs=rows, check_vma=False)
```

```python
import functools

import jax
import jax.numpy as jnp
from jax import lax
from jax.experimental import pallas as pl
from jax.experimental.pallas import tpu as pltpu
from jax.sharding import PartitionSpec as P

ROWS = 16
PAD = 128


def kernel(plan, tokens, routes, codes, wg_hbm, wu_hbm, wd_hbm, out, X, PT, HID, RC, RY, RUP, RDN, wg, wu, wd,
           ag_recv, ag_send, c_send, c_recv, y_send, y_recv, up_send, up_recv, dn_send, dn_recv, w_sem):
    Z, Y, C, Q, D, ag_parts, rs_parts = plan
    ZY = Z * Y
    me = lax.axis_index("hst")
    c = lax.rem(me, C)
    y = lax.rem(lax.div(me, C), Y)
    z = lax.div(me, C * Y)
    oc = 1 - c
    oy = 1 - y

    def dev(zz, yy, cc):
        return (zz * Y + yy) * C + cc

    def blk(zz, yy):
        return zz * Y + yy

    def at(q, cc, b):
        return pl.ds(pl.multiple_of(((q * C + cc) * ZY + b) * ROWS, ROWS), ROWS)

    def slot(q, b, count):
        return pl.ds(pl.multiple_of((q * count + b) * ROWS, ROWS), ROWS)

    has_up = z < Z - 1
    has_dn = z > 0

    def when(cond, fn):
        if cond is None:
            fn()
        else:
            pl.when(cond)(fn)

    def both(a, b):
        return b if a is None else (a if b is None else jnp.logical_and(a, b))

    pending = []

    def remote(src, dst, ssem, rsem, to):
        return pltpu.make_async_remote_copy(src_ref=src, dst_ref=dst, send_sem=ssem, recv_sem=rsem,
                                            device_id={"hst": to}, device_id_type=pl.DeviceIdType.MESH)

    def send(cond, make):
        when(cond, lambda: make().start())
        pending.append((cond, make))

    loads = [pltpu.make_async_copy(a, b, w_sem.at[i]) for i, (a, b) in
             enumerate(((wg_hbm, wg), (wu_hbm, wu), (wd_hbm, wd)))]
    for load in loads:
        load.start()

    barrier = pltpu.get_barrier_semaphore()

    def greet(to):
        pl.semaphore_signal(barrier, inc=1, device_id={"hst": to}, device_id_type=pl.DeviceIdType.MESH)

    greet(dev(z, y, oc))
    if Y > 1:
        greet(dev(z, oy, c))
    pl.when(has_up)(lambda: greet(dev(z + 1, y, c)))
    pl.when(has_dn)(lambda: greet(dev(z - 1, y, c)))

    lane = lax.broadcasted_iota(jnp.int32, (Q * ROWS, PAD), 1)
    half = PAD // 2
    expert = lax.rem(lane, half)
    total = jnp.zeros((Q * ROWS, 1), jnp.float32)
    weight = jnp.zeros((Q * ROWS, PAD), jnp.float32)
    for k in range(routes.shape[1]):
        code = codes[:, k:k + 1].astype(jnp.float32)
        total = total + code
        weight = weight + jnp.where(expert == routes[:, k:k + 1], code, 0.0)
    weight = weight / total
    high = weight.astype(jnp.bfloat16).astype(jnp.float32)
    packed = jnp.where(lane < half, high, weight - high).astype(jnp.bfloat16)
    for q in range(Q):
        X[at(q, c, blk(z, y)), 0:D] = tokens[q * ROWS:(q + 1) * ROWS, :]
        X[at(q, c, blk(z, y)), D:D + PAD] = packed[q * ROWS:(q + 1) * ROWS, :]
    pl.semaphore_wait(barrier, 1 + (Y - 1) + has_up.astype(jnp.int32) + has_dn.astype(jnp.int32))

    def ag_send_one(q, p, kind, cc, b, to, cond):
        c0, c1, _ = ag_parts[p]

        def make():
            ref = X.at[at(q, cc, b), c0:c1]
            return remote(ref, ref, ag_send.at[q, p, kind, b], ag_recv.at[q, p, cc * ZY + b], to)
        send(cond, make)

    def ag_wait(q, p, cc, b, cond):
        c0, c1, _ = ag_parts[p]

        def fn():
            ref = X.at[at(q, cc, b), c0:c1]
            remote(ref, ref, ag_send.at[q, p, 0, b], ag_recv.at[q, p, cc * ZY + b], dev(z, y, oc)).wait_recv()
        when(cond, fn)

    def go_up(q, p, b, cond=None):
        ag_send_one(q, p, 0, c, b, dev(z + 1, y, c), both(cond, has_up))

    def go_dn(q, p, b, cond=None):
        ag_send_one(q, p, 1, c, b, dev(z - 1, y, c), both(cond, has_dn))

    def go_y(q, p, b, cond=None):
        ag_send_one(q, p, 2, c, b, dev(z, oy, c), cond)

    def go_c(q, p, b, cond=None):
        ag_send_one(q, p, 3, c, b, dev(z, y, oc), cond)

    def ag_start(q):
        for p, (_, _, first) in enumerate(ag_parts):
            own = blk(z, y)
            if Y > 1:
                go_y(q, p, own)
            go_up(q, p, own)
            go_dn(q, p, own)
            go_c(q, p, own)

    def ag_turn(q):
        for p, (_, _, first) in enumerate(ag_parts):
            if first == "y":
                b = blk(z, oy)
                ag_wait(q, p, c, b, None)
                go_up(q, p, b)
                go_dn(q, p, b)
                go_c(q, p, b)

    def ag_step(q, s):
        for p, (_, _, first) in enumerate(ag_parts):
            for yy in ((y, oy) if first == "y" else (y,)):
                lo, hi = z - s, z + s
                ok_lo, ok_hi = lo >= 0, hi < Z
                ag_wait(q, p, c, blk(lo, yy), ok_lo)
                go_up(q, p, blk(lo, yy), ok_lo)
                if first == "z" and Y > 1:
                    go_y(q, p, blk(lo, yy), ok_lo)
                ag_wait(q, p, c, blk(hi, yy), ok_hi)
                go_dn(q, p, blk(hi, yy), ok_hi)
                if first == "z" and Y > 1:
                    go_y(q, p, blk(hi, yy), ok_hi)
                go_c(q, p, blk(lo, yy), ok_lo)
                go_c(q, p, blk(hi, yy), ok_hi)

    def ag_cross(q, s):
        for p, (_, _, first) in enumerate(ag_parts):
            if first == "z" and Y > 1:
                if s == 0:
                    ag_wait(q, p, c, blk(z, oy), None)
                    go_c(q, p, blk(z, oy))
                else:
                    for far, ok in ((z - s, z - s >= 0), (z + s, z + s < Z)):
                        ag_wait(q, p, c, blk(far, oy), ok)
                        go_c(q, p, blk(far, oy), ok)

    def ag_end(q):
        for p in range(len(ag_parts)):
            for b in range(ZY):
                ag_wait(q, p, oc, b, None)

    rows_all = C * ZY * ROWS
    F = wg.shape[1]
    tile_f = 256 if F % 256 == 0 else F
    tile_d = 512

    def gate_up(q, j):
        cols = slice(j * tile_f, (j + 1) * tile_f)
        rows = X[q * rows_all:(q + 1) * rows_all, 0:D]
        g = jnp.dot(rows, wg[:, cols], preferred_element_type=jnp.float32)
        u = jnp.dot(rows, wu[:, cols], preferred_element_type=jnp.float32)
        HID[:, cols] = (g / (1.0 + jnp.exp(-g)) * u).astype(jnp.bfloat16)

    def down(q, d0, d1):
        lanes = lax.broadcasted_iota(jnp.int32, (rows_all, PAD), 1)
        both_parts = X[q * rows_all:(q + 1) * rows_all, D:D + PAD].astype(jnp.float32)
        col = jnp.sum(jnp.where(lax.rem(lanes, half) == me, both_parts, 0.0), axis=1, keepdims=True)

        def body(i, carry):
            cols = pl.ds(pl.multiple_of(i * tile_d, tile_d), tile_d)
            o = jnp.dot(HID[...], wd[:, cols], preferred_element_type=jnp.float32)
            PT[q * rows_all:(q + 1) * rows_all, cols] = (o * col).astype(jnp.bfloat16)
            return carry
        lax.fori_loop(d0 // tile_d, d1 // tile_d, body, 0)

    def c_copy(q, p):
        c0, c1, _ = rs_parts[p]
        src = PT.at[pl.ds(pl.multiple_of((q * C + oc) * ZY * ROWS, ROWS), ZY * ROWS), c0:c1]
        dst = RC.at[q * ZY * ROWS:(q + 1) * ZY * ROWS, c0:c1]
        return remote(src, dst, c_send.at[q, p], c_recv.at[q, p], dev(z, y, oc))

    def y_copy(q, p, b, zz):
        c0, c1, _ = rs_parts[p]
        return remote(PT.at[at(q, c, b), c0:c1], RY.at[slot(q, zz, Z), c0:c1],
                      y_send.at[q, p, zz], y_recv.at[q, p, zz], dev(z, oy, c))

    def up_copy(q, p, b):
        c0, c1, _ = rs_parts[p]
        return remote(PT.at[at(q, c, b), c0:c1], RUP.at[slot(q, b, ZY), c0:c1],
                      up_send.at[q, p, b], up_recv.at[q, p, b], dev(z + 1, y, c))

    def dn_copy(q, p, b):
        c0, c1, _ = rs_parts[p]
        return remote(PT.at[at(q, c, b), c0:c1], RDN.at[slot(q, b, ZY), c0:c1],
                      dn_send.at[q, p, b], dn_recv.at[q, p, b], dev(z - 1, y, c))

    def add(p, dst, dst_rows, terms):
        c0, c1, _ = rs_parts[p]
        tile = 512 if (c1 - c0) % 512 == 0 and c0 % 512 == 0 else 128

        def body(i, carry):
            cols = pl.ds(pl.multiple_of(i * tile, tile), tile)
            s = terms[0][0][terms[0][1], cols].astype(jnp.float32)
            for ref, r in terms[1:]:
                s = s + ref[r, cols].astype(jnp.float32)
            dst[dst_rows, cols] = s.astype(jnp.bfloat16)
            return carry
        lax.fori_loop(c0 // tile, c1 // tile, body, 0)

    def rs_start(q):
        for p in range(len(rs_parts)):
            send(None, lambda p=p: c_copy(q, p))

    def rs_sibling(q):
        for p, (_, _, last) in enumerate(rs_parts):
            c_copy(q, p).wait_recv()

    def rs_cross(q, s):
        for p, (_, _, last) in enumerate(rs_parts):
            if last == "z" and Y > 1:
                for zz, ok in (((z - s, z - s >= 0), (z + s, z + s < Z)) if s else ((z, None),)):
                    b = blk(zz, oy)
                    when(ok, lambda b=b, p=p: add(p, PT, at(q, c, b), [(PT, at(q, c, b)), (RC, slot(q, b, ZY))]))
                    send(ok, lambda b=b, p=p, zz=zz: y_copy(q, p, b, zz))

    def base_terms(q, p, b, zz):
        terms = [(PT, at(q, c, b)), (RC, slot(q, b, ZY))]
        if rs_parts[p][2] == "z" and Y > 1:
            y_copy(q, p, b, zz).wait_recv()
            terms.append((RY, slot(q, zz, Z)))
        return terms

    def rs_step(q, s):
        for p, (_, _, last) in enumerate(rs_parts):
            for yy in ((oy, y) if last == "y" else (y,)):
                for far, ok, more, copy, R in ((z - s, z - s >= 0, has_up, dn_copy, RDN),
                                               (z + s, z + s < Z, has_dn, up_copy, RUP)):
                    b = blk(far, yy)

                    def fn(b=b, p=p, far=far, more=more, copy=copy, R=R):
                        terms = base_terms(q, p, b, far)

                        @pl.when(more)
                        def _():
                            copy(q, p, b).wait_recv()
                            add(p, PT, at(q, c, b), terms + [(R, slot(q, b, ZY))])

                        @pl.when(jnp.logical_not(more))
                        def _():
                            add(p, PT, at(q, c, b), terms)
                    when(ok, fn)
                    send(ok, lambda b=b, p=p, copy=copy: copy(q, p, b))

    def rs_final(q):
        for p, (_, _, last) in enumerate(rs_parts):
            for yy in ((oy, y) if last == "y" else (y,)):
                b = blk(z, yy)
                terms = base_terms(q, p, b, z)
                pl.when(has_up)(lambda p=p, b=b: dn_copy(q, p, b).wait_recv())
                pl.when(has_dn)(lambda p=p, b=b: up_copy(q, p, b).wait_recv())
                up_term, dn_term = (RUP, slot(q, b, ZY)), (RDN, slot(q, b, ZY))
                if last == "y":
                    dst, dst_rows = PT, at(q, c, b)
                else:
                    dst, dst_rows = out, slice(q * ROWS, (q + 1) * ROWS)
                pl.when(jnp.logical_and(has_up, has_dn))(
                    lambda p=p, t=terms, u=up_term, d=dn_term, a=dst, r=dst_rows: add(p, a, r, t + [u, d]))
                pl.when(jnp.logical_not(has_up))(
                    lambda p=p, t=terms, u=up_term, a=dst, r=dst_rows: add(p, a, r, t + [u]))
                pl.when(jnp.logical_not(has_dn))(
                    lambda p=p, t=terms, d=dn_term, a=dst, r=dst_rows: add(p, a, r, t + [d]))
                if last == "y" and yy is oy:
                    send(None, lambda p=p, b=b: y_copy(q, p, b, z))

    def rs_last(q):
        for p, (_, _, last) in enumerate(rs_parts):
            if last == "y":
                b = blk(z, y)
                y_copy(q, p, b, z).wait_recv()
                add(p, out, slice(q * ROWS, (q + 1) * ROWS), [(PT, at(q, c, b)), (RY, slot(q, z, Z))])

    def ag_list(q):
        return ([lambda: ag_start(q), lambda: ag_turn(q)]
                + [lambda s=s: ag_step(q, s) for s in range(1, Z)]
                + [lambda s=s: ag_cross(q, s) for s in range(Z)] + [lambda: ag_end(q)])

    def ffn_list(q):
        def first(j):
            if q == 0 and j == 0:
                loads[0].wait()
                loads[1].wait()
            gate_up(q, j)

        def last(d0, d1):
            if q == 0 and d0 == 0:
                loads[2].wait()
            down(q, d0, d1)
        return [lambda j=j: first(j) for j in range(F // tile_f)] + [lambda: last(0, D)]

    def rs_list(q):
        return ([lambda: rs_start(q), lambda: rs_sibling(q)]
                + [lambda s=s: rs_cross(q, s) for s in range(Z - 1, -1, -1)]
                + [lambda s=s: rs_step(q, s) for s in range(Z - 1, 0, -1)]
                + [lambda: rs_final(q), lambda: rs_last(q)])

    def run(*lists):
        longest = max(len(a) for a in lists)
        places = []
        for n, a in enumerate(lists):
            places += [((i + 1) / (len(a) + 1), n, f) for i, f in enumerate(a)]
        for _, _, f in sorted(places, key=lambda t: t[:2]):
            f()
        del longest

    run(ag_list(0))
    for q in range(Q):
        if q + 1 < Q:
            run(ag_list(q + 1), ffn_list(q)) if q == 0 else run(ag_list(q + 1), ffn_list(q), rs_list(q - 1))
        elif q:
            run(ffn_list(q), rs_list(q - 1))
        else:
            run(ffn_list(q))
    run(rs_list(Q - 1))
    for cond, make in pending:
        when(cond, lambda make=make: make().wait_send())


def local(shape, tokens, routes, gate_code, w_gate, w_up, w_down):
    Z, Y, C, ag_cut, rs_cut = shape
    n = Z * Y * C
    rows, D = tokens.shape
    F = w_gate.shape[2]
    Q = rows // ROWS
    wide = D + PAD
    ag_parts = tuple((a, b, m) for a, b, m in ((0, ag_cut, "y"), (ag_cut, wide, "z")) if b > a)
    rs_parts = tuple((a, b, m) for a, b, m in ((0, rs_cut, "y"), (rs_cut, D, "z")) if b > a)
    NA, NR, ZY = len(ag_parts), len(rs_parts), Z * Y
    plan = (Z, Y, C, Q, D, ag_parts, rs_parts)
    bf = jnp.bfloat16
    dma = pltpu.SemaphoreType.DMA
    vmem = pl.BlockSpec(memory_space=pltpu.VMEM)
    hbm = pl.BlockSpec(memory_space=pl.ANY)
    z_rows = Q * ZY * ROWS
    return pl.pallas_call(
        functools.partial(kernel, plan),
        out_shape=jax.ShapeDtypeStruct((rows, D), bf),
        in_specs=[vmem, vmem, vmem, hbm, hbm, hbm],
        out_specs=vmem,
        scratch_shapes=[
            pltpu.VMEM((Q * n * ROWS, wide), bf),
            pltpu.VMEM((Q * n * ROWS, D), bf),
            pltpu.VMEM((n * ROWS, F), bf),
            pltpu.VMEM((z_rows, D), bf),
            pltpu.VMEM((Q * Z * ROWS, D), bf),
            pltpu.VMEM((z_rows, D), bf),
            pltpu.VMEM((z_rows, D), bf),
            pltpu.VMEM((D, F), bf),
            pltpu.VMEM((D, F), bf),
            pltpu.VMEM((F, D), bf),
            dma((Q, NA, n)), dma((Q, NA, 4, ZY)),
            dma((Q, NR)), dma((Q, NR)),
            dma((Q, NR, Z)), dma((Q, NR, Z)),
            dma((Q, NR, ZY)), dma((Q, NR, ZY)),
            dma((Q, NR, ZY)), dma((Q, NR, ZY)),
            dma((3,)),
        ],
        compiler_params=pltpu.CompilerParams(
            collective_id=0, has_side_effects=True, vmem_limit_bytes=60 * 1024 * 1024),
    )(tokens, routes, gate_code, w_gate[0], w_up[0], w_down[0])


def solution(mesh):
    n = mesh.shape["hst"]
    C = 2
    Y = 2 if n <= 16 else 1
    shape = (n // (C * Y), Y, C, AG_CUT if Y > 1 else 0, RS_CUT if Y > 1 else 0)
    rows = P(("group", "hst"), None)
    whole = P("hst", None, None)
    return jax.shard_map(functools.partial(local, shape), mesh=mesh,
                         in_specs=(rows, rows, rows, whole, whole, whole), out_specs=rows, check_vma=False)


AG_CUT = 1536
RS_CUT = 1536
```

```python
import functools

import jax
import jax.numpy as jnp
from jax import lax
from jax.experimental import pallas as pl
from jax.experimental.pallas import tpu as pltpu
from jax.sharding import PartitionSpec as P

ROWS = 16
PAD = 128


def kernel(plan, tokens, routes, codes, wg_hbm, wu_hbm, wd_hbm, out, X, PT, HID, RC, RY, RUP, RDN, wg, wu, wd,
           ag_recv, ag_send, c_send, c_recv, y_send, y_recv, up_send, up_recv, dn_send, dn_recv, w_sem):
    Z, Y, C, Q, D, ag_parts, rs_parts = plan
    ZY = Z * Y
    me = lax.axis_index("hst")
    c = lax.rem(me, C)
    y = lax.rem(lax.div(me, C), Y)
    z = lax.div(me, C * Y)
    oc = 1 - c
    oy = 1 - y

    def dev(zz, yy, cc):
        return (zz * Y + yy) * C + cc

    def blk(zz, yy):
        return zz * Y + yy

    def at(q, cc, b):
        return pl.ds(pl.multiple_of(((q * C + cc) * ZY + b) * ROWS, ROWS), ROWS)

    def slot(q, b, count):
        return pl.ds(pl.multiple_of((q * count + b) * ROWS, ROWS), ROWS)

    has_up = z < Z - 1
    has_dn = z > 0

    def when(cond, fn):
        if cond is None:
            fn()
        else:
            pl.when(cond)(fn)

    def both(a, b):
        return b if a is None else (a if b is None else jnp.logical_and(a, b))

    pending = []

    def remote(src, dst, ssem, rsem, to):
        return pltpu.make_async_remote_copy(src_ref=src, dst_ref=dst, send_sem=ssem, recv_sem=rsem,
                                            device_id={"hst": to}, device_id_type=pl.DeviceIdType.MESH)

    def send(cond, make):
        when(cond, lambda: make().start())
        pending.append((cond, make))

    loads = [pltpu.make_async_copy(a, b, w_sem.at[i]) for i, (a, b) in
             enumerate(((wg_hbm, wg), (wu_hbm, wu), (wd_hbm, wd)))]
    for load in loads:
        load.start()

    barrier = pltpu.get_barrier_semaphore()

    def greet(to):
        pl.semaphore_signal(barrier, inc=1, device_id={"hst": to}, device_id_type=pl.DeviceIdType.MESH)

    greet(dev(z, y, oc))
    if Y > 1:
        greet(dev(z, oy, c))
    pl.when(has_up)(lambda: greet(dev(z + 1, y, c)))
    pl.when(has_dn)(lambda: greet(dev(z - 1, y, c)))

    half = PAD // 2
    spot = lax.broadcasted_iota(jnp.int32, (PAD, Q * ROWS), 0)
    expert = lax.rem(spot, half)
    total = jnp.zeros((1, Q * ROWS), jnp.float32)
    weight = jnp.zeros((PAD, Q * ROWS), jnp.float32)
    for k in range(routes.shape[0]):
        code = codes[k:k + 1, :].astype(jnp.float32)
        total = total + code
        weight = weight + jnp.where(expert == routes[k:k + 1, :], code, 0.0)
    weight = weight / total
    high = weight.astype(jnp.bfloat16).astype(jnp.float32)
    columns = jnp.where(spot < half, high, weight - high).astype(jnp.bfloat16)
    same = (lax.broadcasted_iota(jnp.int32, (Q * ROWS, Q * ROWS), 0)
            == lax.broadcasted_iota(jnp.int32, (Q * ROWS, Q * ROWS), 1)).astype(jnp.float32).astype(jnp.bfloat16)
    packed = lax.dot_general(same, columns, (((1,), (1,)), ((), ())),
                             preferred_element_type=jnp.float32).astype(jnp.bfloat16)
    for q in range(Q):
        X[at(q, c, blk(z, y)), 0:D] = tokens[q * ROWS:(q + 1) * ROWS, :]
        X[at(q, c, blk(z, y)), D:D + PAD] = packed[q * ROWS:(q + 1) * ROWS, :]
    pl.semaphore_wait(barrier, 1 + (Y - 1) + has_up.astype(jnp.int32) + has_dn.astype(jnp.int32))

    def ag_send_one(q, p, kind, cc, b, to, cond):
        c0, c1, _ = ag_parts[p]

        def make():
            ref = X.at[at(q, cc, b), c0:c1]
            return remote(ref, ref, ag_send.at[q, p, kind, b], ag_recv.at[q, p, cc * ZY + b], to)
        send(cond, make)

    def ag_wait(q, p, cc, b, cond):
        c0, c1, _ = ag_parts[p]

        def fn():
            ref = X.at[at(q, cc, b), c0:c1]
            remote(ref, ref, ag_send.at[q, p, 0, b], ag_recv.at[q, p, cc * ZY + b], dev(z, y, oc)).wait_recv()
        when(cond, fn)

    def go_up(q, p, b, cond=None):
        ag_send_one(q, p, 0, c, b, dev(z + 1, y, c), both(cond, has_up))

    def go_dn(q, p, b, cond=None):
        ag_send_one(q, p, 1, c, b, dev(z - 1, y, c), both(cond, has_dn))

    def go_y(q, p, b, cond=None):
        ag_send_one(q, p, 2, c, b, dev(z, oy, c), cond)

    def go_c(q, p, b, cond=None):
        ag_send_one(q, p, 3, c, b, dev(z, y, oc), cond)

    def ag_start(q):
        for p, (_, _, first) in enumerate(ag_parts):
            own = blk(z, y)
            if Y > 1:
                go_y(q, p, own)
            go_up(q, p, own)
            go_dn(q, p, own)
            go_c(q, p, own)

    def ag_turn(q):
        for p, (_, _, first) in enumerate(ag_parts):
            if first == "y":
                b = blk(z, oy)
                ag_wait(q, p, c, b, None)
                go_up(q, p, b)
                go_dn(q, p, b)
                go_c(q, p, b)

    def ag_step(q, s):
        for p, (_, _, first) in enumerate(ag_parts):
            for yy in ((y, oy) if first == "y" else (y,)):
                lo, hi = z - s, z + s
                ok_lo, ok_hi = lo >= 0, hi < Z
                ag_wait(q, p, c, blk(lo, yy), ok_lo)
                go_up(q, p, blk(lo, yy), ok_lo)
                if first == "z" and Y > 1:
                    go_y(q, p, blk(lo, yy), ok_lo)
                ag_wait(q, p, c, blk(hi, yy), ok_hi)
                go_dn(q, p, blk(hi, yy), ok_hi)
                if first == "z" and Y > 1:
                    go_y(q, p, blk(hi, yy), ok_hi)
                go_c(q, p, blk(lo, yy), ok_lo)
                go_c(q, p, blk(hi, yy), ok_hi)

    def ag_cross(q, s):
        for p, (_, _, first) in enumerate(ag_parts):
            if first == "z" and Y > 1:
                if s == 0:
                    ag_wait(q, p, c, blk(z, oy), None)
                    go_c(q, p, blk(z, oy))
                else:
                    for far, ok in ((z - s, z - s >= 0), (z + s, z + s < Z)):
                        ag_wait(q, p, c, blk(far, oy), ok)
                        go_c(q, p, blk(far, oy), ok)

    def ag_end(q):
        for p in range(len(ag_parts)):
            for b in range(ZY):
                ag_wait(q, p, oc, b, None)

    rows_all = C * ZY * ROWS
    F = wg.shape[1]
    tile_f = 256 if F % 256 == 0 else F
    tile_d = 512

    def gate_up(q, j):
        cols = slice(j * tile_f, (j + 1) * tile_f)
        rows = X[q * rows_all:(q + 1) * rows_all, 0:D]
        g = jnp.dot(rows, wg[:, cols], preferred_element_type=jnp.float32)
        u = jnp.dot(rows, wu[:, cols], preferred_element_type=jnp.float32)
        HID[:, cols] = (g / (1.0 + jnp.exp(-g)) * u).astype(jnp.bfloat16)

    def down(q, d0, d1):
        lanes = lax.broadcasted_iota(jnp.int32, (rows_all, PAD), 1)
        both_parts = X[q * rows_all:(q + 1) * rows_all, D:D + PAD].astype(jnp.float32)
        col = jnp.sum(jnp.where(lax.rem(lanes, half) == me, both_parts, 0.0), axis=1, keepdims=True)

        def body(i, carry):
            cols = pl.ds(pl.multiple_of(i * tile_d, tile_d), tile_d)
            o = jnp.dot(HID[...], wd[:, cols], preferred_element_type=jnp.float32)
            PT[q * rows_all:(q + 1) * rows_all, cols] = (o * col).astype(jnp.bfloat16)
            return carry
        lax.fori_loop(d0 // tile_d, d1 // tile_d, body, 0)

    def c_copy(q, p):
        c0, c1, _ = rs_parts[p]
        src = PT.at[pl.ds(pl.multiple_of((q * C + oc) * ZY * ROWS, ROWS), ZY * ROWS), c0:c1]
        dst = RC.at[q * ZY * ROWS:(q + 1) * ZY * ROWS, c0:c1]
        return remote(src, dst, c_send.at[q, p], c_recv.at[q, p], dev(z, y, oc))

    def y_copy(q, p, b, zz):
        c0, c1, _ = rs_parts[p]
        return remote(PT.at[at(q, c, b), c0:c1], RY.at[slot(q, zz, Z), c0:c1],
                      y_send.at[q, p, zz], y_recv.at[q, p, zz], dev(z, oy, c))

    def up_copy(q, p, b):
        c0, c1, _ = rs_parts[p]
        return remote(PT.at[at(q, c, b), c0:c1], RUP.at[slot(q, b, ZY), c0:c1],
                      up_send.at[q, p, b], up_recv.at[q, p, b], dev(z + 1, y, c))

    def dn_copy(q, p, b):
        c0, c1, _ = rs_parts[p]
        return remote(PT.at[at(q, c, b), c0:c1], RDN.at[slot(q, b, ZY), c0:c1],
                      dn_send.at[q, p, b], dn_recv.at[q, p, b], dev(z - 1, y, c))

    def add(p, dst, dst_rows, terms):
        c0, c1, _ = rs_parts[p]
        tile = 512 if (c1 - c0) % 512 == 0 and c0 % 512 == 0 else 128

        def body(i, carry):
            cols = pl.ds(pl.multiple_of(i * tile, tile), tile)
            s = terms[0][0][terms[0][1], cols].astype(jnp.float32)
            for ref, r in terms[1:]:
                s = s + ref[r, cols].astype(jnp.float32)
            dst[dst_rows, cols] = s.astype(jnp.bfloat16)
            return carry
        lax.fori_loop(c0 // tile, c1 // tile, body, 0)

    def rs_start(q):
        for p in range(len(rs_parts)):
            send(None, lambda p=p: c_copy(q, p))

    def rs_sibling(q):
        for p, (_, _, last) in enumerate(rs_parts):
            c_copy(q, p).wait_recv()

    def rs_cross(q, s):
        for p, (_, _, last) in enumerate(rs_parts):
            if last == "z" and Y > 1:
                for zz, ok in (((z - s, z - s >= 0), (z + s, z + s < Z)) if s else ((z, None),)):
                    b = blk(zz, oy)
                    when(ok, lambda b=b, p=p: add(p, PT, at(q, c, b), [(PT, at(q, c, b)), (RC, slot(q, b, ZY))]))
                    send(ok, lambda b=b, p=p, zz=zz: y_copy(q, p, b, zz))

    def base_terms(q, p, b, zz):
        terms = [(PT, at(q, c, b)), (RC, slot(q, b, ZY))]
        if rs_parts[p][2] == "z" and Y > 1:
            y_copy(q, p, b, zz).wait_recv()
            terms.append((RY, slot(q, zz, Z)))
        return terms

    def rs_step(q, s, only):
        for p, (_, _, last) in enumerate(rs_parts):
            if p != only:
                continue
            for yy in ((oy, y) if last == "y" else (y,)):
                for far, ok, more, copy, R in ((z - s, z - s >= 0, has_up, dn_copy, RDN),
                                               (z + s, z + s < Z, has_dn, up_copy, RUP)):
                    b = blk(far, yy)

                    def fn(b=b, p=p, far=far, more=more, copy=copy, R=R):
                        terms = base_terms(q, p, b, far)

                        @pl.when(more)
                        def _():
                            copy(q, p, b).wait_recv()
                            add(p, PT, at(q, c, b), terms + [(R, slot(q, b, ZY))])

                        @pl.when(jnp.logical_not(more))
                        def _():
                            add(p, PT, at(q, c, b), terms)
                    when(ok, fn)
                    send(ok, lambda b=b, p=p, copy=copy: copy(q, p, b))

    def rs_final(q):
        for p, (_, _, last) in enumerate(rs_parts):
            for yy in ((oy, y) if last == "y" else (y,)):
                b = blk(z, yy)
                terms = base_terms(q, p, b, z)
                pl.when(has_up)(lambda p=p, b=b: dn_copy(q, p, b).wait_recv())
                pl.when(has_dn)(lambda p=p, b=b: up_copy(q, p, b).wait_recv())
                up_term, dn_term = (RUP, slot(q, b, ZY)), (RDN, slot(q, b, ZY))
                if last == "y":
                    dst, dst_rows = PT, at(q, c, b)
                else:
                    dst, dst_rows = out, slice(q * ROWS, (q + 1) * ROWS)
                pl.when(jnp.logical_and(has_up, has_dn))(
                    lambda p=p, t=terms, u=up_term, d=dn_term, a=dst, r=dst_rows: add(p, a, r, t + [u, d]))
                pl.when(jnp.logical_not(has_up))(
                    lambda p=p, t=terms, u=up_term, a=dst, r=dst_rows: add(p, a, r, t + [u]))
                pl.when(jnp.logical_not(has_dn))(
                    lambda p=p, t=terms, d=dn_term, a=dst, r=dst_rows: add(p, a, r, t + [d]))
                if last == "y" and yy is oy:
                    send(None, lambda p=p, b=b: y_copy(q, p, b, z))

    def rs_last(q):
        for p, (_, _, last) in enumerate(rs_parts):
            if last == "y":
                b = blk(z, y)
                y_copy(q, p, b, z).wait_recv()
                add(p, out, slice(q * ROWS, (q + 1) * ROWS), [(PT, at(q, c, b)), (RY, slot(q, z, Z))])

    def ag_list(q):
        events = [lambda: ag_start(q), lambda: ag_turn(q)]
        for s in range(1, Z):
            events += [lambda s=s: ag_step(q, s), lambda s=s: ag_cross(q, s - 1)]
        return events + [lambda: ag_cross(q, Z - 1), lambda: ag_end(q)]

    def ffn_list(q):
        def first(j):
            if q == 0 and j == 0:
                loads[0].wait()
                loads[1].wait()
            gate_up(q, j)

        def last(d0, d1):
            if q == 0 and d0 == 0:
                loads[2].wait()
            down(q, d0, d1)
        return [lambda j=j: first(j) for j in range(F // tile_f)] + [lambda: last(0, D // 2), lambda: last(D // 2, D)]

    def rs_list(q):
        parts = range(len(rs_parts))
        events = [lambda: rs_sibling(q)]
        for s in range(Z - 1, -1, -1):
            events.append(lambda s=s: rs_cross(q, s))
        for n, s in enumerate(range(Z - 1, 0, -1)):
            for p in parts:
                place = 2 + n + 2 * (n + 1) if rs_parts[p][2] == "z" else 2 + 2 * n + n
                events.insert(min(place, len(events)), lambda s=s, p=p: rs_step(q, s, p))
        return events + [lambda: rs_final(q), lambda: rs_last(q)]

    def run(*lists):
        places = []
        for n, a in enumerate(lists):
            places += [((i + 1) / (len(a) + 1), n, f) for i, f in enumerate(a)]
        for _, _, f in sorted(places, key=lambda e: e[:2]):
            f()

    def lagged(a, b, lag):
        for i in range(max(len(a), len(b) + lag)):
            if i < len(a):
                a[i]()
            if 0 <= i - lag < len(b):
                b[i - lag]()

    ahead = ag_list(0)
    later = ag_list(1) if Q > 1 else []
    lagged(ahead, later[:len(ahead) - AG_LAG], AG_LAG)
    later = later[len(ahead) - AG_LAG:]
    before = []
    for q in range(Q):
        k = min(RS_EARLY, len(before))
        run(ffn_list(q), later if q == 0 else before[:k])
        rs_start(q)
        if q == 0:
            before = rs_list(0)
        else:
            if q + 1 < Q:
                run(ag_list(q + 1), before[k:])
                before = rs_list(q)
            else:
                lagged(before[k:], rs_list(q), RS_LAG)
                before = []
    run(before)
    for cond, make in pending:
        when(cond, lambda make=make: make().wait_send())


def local(shape, tokens, routes, gate_code, w_gate, w_up, w_down):
    Z, Y, C, ag_cut, rs_cut = shape
    n = Z * Y * C
    rows, D = tokens.shape
    F = w_gate.shape[2]
    Q = rows // ROWS
    wide = D + PAD
    ag_parts = tuple((a, b, m) for a, b, m in ((0, ag_cut, "y"), (ag_cut, wide, "z")) if b > a)
    rs_parts = tuple((a, b, m) for a, b, m in ((0, rs_cut, "y"), (rs_cut, D, "z")) if b > a)
    NA, NR, ZY = len(ag_parts), len(rs_parts), Z * Y
    plan = (Z, Y, C, Q, D, ag_parts, rs_parts)
    bf = jnp.bfloat16
    dma = pltpu.SemaphoreType.DMA
    vmem = pl.BlockSpec(memory_space=pltpu.VMEM)
    hbm = pl.BlockSpec(memory_space=pl.ANY)
    z_rows = Q * ZY * ROWS
    return pl.pallas_call(
        functools.partial(kernel, plan),
        out_shape=jax.ShapeDtypeStruct((rows, D), bf),
        in_specs=[vmem, vmem, vmem, hbm, hbm, hbm],
        out_specs=vmem,
        scratch_shapes=[
            pltpu.VMEM((Q * n * ROWS, wide), bf),
            pltpu.VMEM((Q * n * ROWS, D), bf),
            pltpu.VMEM((n * ROWS, F), bf),
            pltpu.VMEM((z_rows, D), bf),
            pltpu.VMEM((Q * Z * ROWS, D), bf),
            pltpu.VMEM((z_rows, D), bf),
            pltpu.VMEM((z_rows, D), bf),
            pltpu.VMEM((D, F), bf),
            pltpu.VMEM((D, F), bf),
            pltpu.VMEM((F, D), bf),
            dma((Q, NA, n)), dma((Q, NA, 4, ZY)),
            dma((Q, NR)), dma((Q, NR)),
            dma((Q, NR, Z)), dma((Q, NR, Z)),
            dma((Q, NR, ZY)), dma((Q, NR, ZY)),
            dma((Q, NR, ZY)), dma((Q, NR, ZY)),
            dma((3,)),
        ],
        compiler_params=pltpu.CompilerParams(
            collective_id=0, has_side_effects=True, vmem_limit_bytes=60 * 1024 * 1024),
    )(tokens, routes.T, gate_code.T, w_gate[0], w_up[0], w_down[0])


def solution(mesh):
    n = mesh.shape["hst"]
    C = 2
    Y = 2 if n <= 16 else 1
    shape = (n // (C * Y), Y, C, AG_CUT if Y > 1 else 0, RS_CUT if Y > 1 else 0)
    rows = P(("group", "hst"), None)
    whole = P("hst", None, None)
    return jax.shard_map(functools.partial(local, shape), mesh=mesh,
                         in_specs=(rows, rows, rows, whole, whole, whole), out_specs=rows, check_vma=False)


AG_CUT = 0
RS_CUT = 512
AG_LAG = 3
RS_EARLY = 5
RS_LAG = 1
```

```python
import functools

import jax
import jax.numpy as jnp
from jax import lax
from jax.experimental import pallas as pl
from jax.experimental.pallas import tpu as pltpu
from jax.sharding import PartitionSpec as P

ROWS = 16
PAD = 128


def kernel(plan, tokens, routes, codes, wg_hbm, wu_hbm, wd_hbm, out, X, PT, HID, RC, RY, RUP, RDN, wg, wu, wd,
           ag_recv, ag_send, c_send, c_recv, y_send, y_recv, up_send, up_recv, dn_send, dn_recv, w_sem):
    Z, Y, C, Q, D, ag_parts, rs_parts = plan
    ZY = Z * Y
    me = lax.axis_index("hst")
    c = lax.rem(me, C)
    y = lax.rem(lax.div(me, C), Y)
    z = lax.div(me, C * Y)
    oc = 1 - c
    oy = 1 - y

    def dev(zz, yy, cc):
        return (zz * Y + yy) * C + cc

    def blk(zz, yy):
        return zz * Y + yy

    def at(q, cc, b):
        return pl.ds(pl.multiple_of(((q * C + cc) * ZY + b) * ROWS, ROWS), ROWS)

    def slot(q, b, count):
        return pl.ds(pl.multiple_of((q * count + b) * ROWS, ROWS), ROWS)

    has_up = z < Z - 1
    has_dn = z > 0

    def when(cond, fn):
        if cond is None:
            fn()
        else:
            pl.when(cond)(fn)

    def both(a, b):
        return b if a is None else (a if b is None else jnp.logical_and(a, b))

    pending = []

    def remote(src, dst, ssem, rsem, to):
        return pltpu.make_async_remote_copy(src_ref=src, dst_ref=dst, send_sem=ssem, recv_sem=rsem,
                                            device_id={"hst": to}, device_id_type=pl.DeviceIdType.MESH)

    def send(cond, make):
        when(cond, lambda: make().start())
        pending.append((cond, make))

    loads = [pltpu.make_async_copy(a, b, w_sem.at[i]) for i, (a, b) in
             enumerate(((wg_hbm, wg), (wu_hbm, wu), (wd_hbm, wd)))]
    for load in loads:
        load.start()

    barrier = pltpu.get_barrier_semaphore()

    def greet(to):
        pl.semaphore_signal(barrier, inc=1, device_id={"hst": to}, device_id_type=pl.DeviceIdType.MESH)

    greet(dev(z, y, oc))
    if Y > 1:
        greet(dev(z, oy, c))
    pl.when(has_up)(lambda: greet(dev(z + 1, y, c)))
    pl.when(has_dn)(lambda: greet(dev(z - 1, y, c)))

    half = PAD // 2
    spot = lax.broadcasted_iota(jnp.int32, (PAD, Q * ROWS), 0)
    expert = lax.rem(spot, half)
    total = jnp.zeros((1, Q * ROWS), jnp.float32)
    weight = jnp.zeros((PAD, Q * ROWS), jnp.float32)
    for k in range(routes.shape[0]):
        code = codes[k:k + 1, :].astype(jnp.float32)
        total = total + code
        weight = weight + jnp.where(expert == routes[k:k + 1, :], code, 0.0)
    weight = weight / total
    high = weight.astype(jnp.bfloat16).astype(jnp.float32)
    columns = jnp.where(spot < half, high, weight - high).astype(jnp.bfloat16)
    same = (lax.broadcasted_iota(jnp.int32, (Q * ROWS, Q * ROWS), 0)
            == lax.broadcasted_iota(jnp.int32, (Q * ROWS, Q * ROWS), 1)).astype(jnp.float32).astype(jnp.bfloat16)
    packed = lax.dot_general(same, columns, (((1,), (1,)), ((), ())),
                             preferred_element_type=jnp.float32).astype(jnp.bfloat16)
    for q in range(Q):
        X[at(q, c, blk(z, y)), 0:D] = tokens[q * ROWS:(q + 1) * ROWS, :]
        X[at(q, c, blk(z, y)), D:D + PAD] = packed[q * ROWS:(q + 1) * ROWS, :]
    pl.semaphore_wait(barrier, 1 + (Y - 1) + has_up.astype(jnp.int32) + has_dn.astype(jnp.int32))

    def ag_send_one(q, p, kind, cc, b, to, cond):
        c0, c1, _ = ag_parts[p]

        def make():
            ref = X.at[at(q, cc, b), c0:c1]
            return remote(ref, ref, ag_send.at[q, p, kind, b], ag_recv.at[q, p, cc * ZY + b], to)
        send(cond, make)

    def ag_wait(q, p, cc, b, cond):
        c0, c1, _ = ag_parts[p]

        def fn():
            ref = X.at[at(q, cc, b), c0:c1]
            remote(ref, ref, ag_send.at[q, p, 0, b], ag_recv.at[q, p, cc * ZY + b], dev(z, y, oc)).wait_recv()
        when(cond, fn)

    def go_up(q, p, b, cond=None):
        ag_send_one(q, p, 0, c, b, dev(z + 1, y, c), both(cond, has_up))

    def go_dn(q, p, b, cond=None):
        ag_send_one(q, p, 1, c, b, dev(z - 1, y, c), both(cond, has_dn))

    def go_y(q, p, b, cond=None):
        ag_send_one(q, p, 2, c, b, dev(z, oy, c), cond)

    def go_c(q, p, b, cond=None):
        ag_send_one(q, p, 3, c, b, dev(z, y, oc), cond)

    def ag_start(q):
        for p, (_, _, first) in enumerate(ag_parts):
            own = blk(z, y)
            if Y > 1:
                go_y(q, p, own)
            go_up(q, p, own)
            go_dn(q, p, own)
            go_c(q, p, own)

    def ag_turn(q):
        for p, (_, _, first) in enumerate(ag_parts):
            if first == "y":
                b = blk(z, oy)
                ag_wait(q, p, c, b, None)
                go_up(q, p, b)
                go_dn(q, p, b)
                go_c(q, p, b)

    def ag_step(q, s):
        for p, (_, _, first) in enumerate(ag_parts):
            for yy in ((y, oy) if first == "y" else (y,)):
                lo, hi = z - s, z + s
                ok_lo, ok_hi = lo >= 0, hi < Z
                ag_wait(q, p, c, blk(lo, yy), ok_lo)
                go_up(q, p, blk(lo, yy), ok_lo)
                if first == "z" and Y > 1:
                    go_y(q, p, blk(lo, yy), ok_lo)
                ag_wait(q, p, c, blk(hi, yy), ok_hi)
                go_dn(q, p, blk(hi, yy), ok_hi)
                if first == "z" and Y > 1:
                    go_y(q, p, blk(hi, yy), ok_hi)
                go_c(q, p, blk(lo, yy), ok_lo)
                go_c(q, p, blk(hi, yy), ok_hi)

    def ag_cross(q, s):
        for p, (_, _, first) in enumerate(ag_parts):
            if first == "z" and Y > 1:
                if s == 0:
                    ag_wait(q, p, c, blk(z, oy), None)
                    go_c(q, p, blk(z, oy))
                else:
                    for far, ok in ((z - s, z - s >= 0), (z + s, z + s < Z)):
                        ag_wait(q, p, c, blk(far, oy), ok)
                        go_c(q, p, blk(far, oy), ok)

    def ag_end(q):
        for p in range(len(ag_parts)):
            for b in range(ZY):
                ag_wait(q, p, oc, b, None)

    rows_all = C * ZY * ROWS
    F = wg.shape[1]
    tile_f = 256 if F % 256 == 0 else F
    tile_d = 512

    def gate_up(q, j):
        cols = slice(j * tile_f, (j + 1) * tile_f)
        rows = X[q * rows_all:(q + 1) * rows_all, 0:D]
        g = jnp.dot(rows, wg[:, cols], preferred_element_type=jnp.float32)
        u = jnp.dot(rows, wu[:, cols], preferred_element_type=jnp.float32)
        HID[:, cols] = (g / (1.0 + jnp.exp(-g)) * u).astype(jnp.bfloat16)

    def down(q, d0, d1):
        lanes = lax.broadcasted_iota(jnp.int32, (rows_all, PAD), 1)
        both_parts = X[q * rows_all:(q + 1) * rows_all, D:D + PAD].astype(jnp.float32)
        col = jnp.sum(jnp.where(lax.rem(lanes, half) == me, both_parts, 0.0), axis=1, keepdims=True)

        def body(i, carry):
            cols = pl.ds(pl.multiple_of(i * tile_d, tile_d), tile_d)
            o = jnp.dot(HID[...], wd[:, cols], preferred_element_type=jnp.float32)
            PT[q * rows_all:(q + 1) * rows_all, cols] = (o * col).astype(jnp.bfloat16)
            return carry
        lax.fori_loop(d0 // tile_d, d1 // tile_d, body, 0)

    def c_copy(q, p):
        c0, c1, _ = rs_parts[p]
        src = PT.at[pl.ds(pl.multiple_of((q * C + oc) * ZY * ROWS, ROWS), ZY * ROWS), c0:c1]
        dst = RC.at[q * ZY * ROWS:(q + 1) * ZY * ROWS, c0:c1]
        return remote(src, dst, c_send.at[q, p], c_recv.at[q, p], dev(z, y, oc))

    def y_copy(q, p, b, zz):
        c0, c1, _ = rs_parts[p]
        return remote(PT.at[at(q, c, b), c0:c1], RY.at[slot(q, zz, Z), c0:c1],
                      y_send.at[q, p, zz], y_recv.at[q, p, zz], dev(z, oy, c))

    def up_copy(q, p, b):
        c0, c1, _ = rs_parts[p]
        return remote(PT.at[at(q, c, b), c0:c1], RUP.at[slot(q, b, ZY), c0:c1],
                      up_send.at[q, p, b], up_recv.at[q, p, b], dev(z + 1, y, c))

    def dn_copy(q, p, b):
        c0, c1, _ = rs_parts[p]
        return remote(PT.at[at(q, c, b), c0:c1], RDN.at[slot(q, b, ZY), c0:c1],
                      dn_send.at[q, p, b], dn_recv.at[q, p, b], dev(z - 1, y, c))

    def add(p, dst, dst_rows, terms):
        c0, c1, _ = rs_parts[p]
        tile = 512 if (c1 - c0) % 512 == 0 and c0 % 512 == 0 else 128

        def body(i, carry):
            cols = pl.ds(pl.multiple_of(i * tile, tile), tile)
            s = terms[0][0][terms[0][1], cols].astype(jnp.float32)
            for ref, r in terms[1:]:
                s = s + ref[r, cols].astype(jnp.float32)
            dst[dst_rows, cols] = s.astype(jnp.bfloat16)
            return carry
        lax.fori_loop(c0 // tile, c1 // tile, body, 0)

    def rs_start(q):
        for p in range(len(rs_parts)):
            send(None, lambda p=p: c_copy(q, p))

    def rs_sibling(q):
        for p, (_, _, last) in enumerate(rs_parts):
            c_copy(q, p).wait_recv()

    def rs_cross(q, s):
        for p, (_, _, last) in enumerate(rs_parts):
            if last == "z" and Y > 1:
                for zz, ok in (((z - s, z - s >= 0), (z + s, z + s < Z)) if s else ((z, None),)):
                    b = blk(zz, oy)
                    when(ok, lambda b=b, p=p: add(p, PT, at(q, c, b), [(PT, at(q, c, b)), (RC, slot(q, b, ZY))]))
                    send(ok, lambda b=b, p=p, zz=zz: y_copy(q, p, b, zz))

    def base_terms(q, p, b, zz):
        terms = [(PT, at(q, c, b)), (RC, slot(q, b, ZY))]
        if rs_parts[p][2] == "z" and Y > 1:
            y_copy(q, p, b, zz).wait_recv()
            terms.append((RY, slot(q, zz, Z)))
        return terms

    def rs_step(q, s, only):
        for p, (_, _, last) in enumerate(rs_parts):
            if p != only:
                continue
            for yy in ((oy, y) if last == "y" else (y,)):
                for far, ok, more, copy, R in ((z - s, z - s >= 0, has_up, dn_copy, RDN),
                                               (z + s, z + s < Z, has_dn, up_copy, RUP)):
                    b = blk(far, yy)

                    def fn(b=b, p=p, far=far, more=more, copy=copy, R=R):
                        terms = base_terms(q, p, b, far)

                        @pl.when(more)
                        def _():
                            copy(q, p, b).wait_recv()
                            add(p, PT, at(q, c, b), terms + [(R, slot(q, b, ZY))])

                        @pl.when(jnp.logical_not(more))
                        def _():
                            add(p, PT, at(q, c, b), terms)
                    when(ok, fn)
                    send(ok, lambda b=b, p=p, copy=copy: copy(q, p, b))

    def rs_final(q):
        for p, (_, _, last) in enumerate(rs_parts):
            for yy in ((oy, y) if last == "y" else (y,)):
                b = blk(z, yy)
                terms = base_terms(q, p, b, z)
                pl.when(has_up)(lambda p=p, b=b: dn_copy(q, p, b).wait_recv())
                pl.when(has_dn)(lambda p=p, b=b: up_copy(q, p, b).wait_recv())
                up_term, dn_term = (RUP, slot(q, b, ZY)), (RDN, slot(q, b, ZY))
                if last == "y":
                    dst, dst_rows = PT, at(q, c, b)
                else:
                    dst, dst_rows = out, slice(q * ROWS, (q + 1) * ROWS)
                pl.when(jnp.logical_and(has_up, has_dn))(
                    lambda p=p, t=terms, u=up_term, d=dn_term, a=dst, r=dst_rows: add(p, a, r, t + [u, d]))
                pl.when(jnp.logical_not(has_up))(
                    lambda p=p, t=terms, u=up_term, a=dst, r=dst_rows: add(p, a, r, t + [u]))
                pl.when(jnp.logical_not(has_dn))(
                    lambda p=p, t=terms, d=dn_term, a=dst, r=dst_rows: add(p, a, r, t + [d]))
                if last == "y" and yy is oy:
                    send(None, lambda p=p, b=b: y_copy(q, p, b, z))

    def rs_last(q):
        for p, (_, _, last) in enumerate(rs_parts):
            if last == "y":
                b = blk(z, y)
                y_copy(q, p, b, z).wait_recv()
                add(p, out, slice(q * ROWS, (q + 1) * ROWS), [(PT, at(q, c, b)), (RY, slot(q, z, Z))])

    def ag_list(q):
        events = [lambda: ag_start(q), lambda: ag_turn(q)]
        for s in range(1, Z):
            events += [lambda s=s: ag_step(q, s), lambda s=s: ag_cross(q, s - 1)]
        return events + [lambda: ag_cross(q, Z - 1), lambda: ag_end(q)]

    def ffn_list(q):
        def first(j):
            if q == 0 and j == 0:
                loads[0].wait()
                loads[1].wait()
            gate_up(q, j)

        def last(d0, d1):
            if q == 0 and d0 == 0:
                loads[2].wait()
            down(q, d0, d1)
        return [lambda j=j: first(j) for j in range(F // tile_f)] + [lambda: last(0, D // 2), lambda: last(D // 2, D)]

    def rs_list(q):
        parts = range(len(rs_parts))
        events = [lambda: rs_sibling(q)]
        for s in range(Z - 1, -1, -1):
            events.append(lambda s=s: rs_cross(q, s))
        for n, s in enumerate(range(Z - 1, 0, -1)):
            for p in parts:
                place = 2 + n + 2 * (n + 1) if rs_parts[p][2] == "z" else 2 + 2 * n + n
                events.insert(min(place, len(events)), lambda s=s, p=p: rs_step(q, s, p))
        return events + [lambda: rs_final(q), lambda: rs_last(q)]

    def run(*lists):
        places = []
        for n, a in enumerate(lists):
            places += [((i + 1) / (len(a) + 1), n, f) for i, f in enumerate(a)]
        for _, _, f in sorted(places, key=lambda e: e[:2]):
            f()

    def lagged(a, b, lag):
        for i in range(max(len(a), len(b) + lag)):
            if i < len(a):
                a[i]()
            if 0 <= i - lag < len(b):
                b[i - lag]()

    ahead = ag_list(0)
    later = ag_list(1) if Q > 1 else []
    lagged(ahead, later[:len(ahead) - AG_LAG], AG_LAG)
    later = later[len(ahead) - AG_LAG:]
    before = []
    for q in range(Q):
        k = min(RS_EARLY, len(before))
        run(ffn_list(q), later if q == 0 else before[:k])
        rs_start(q)
        if q == 0:
            before = rs_list(0)
        else:
            if q + 1 < Q:
                run(ag_list(q + 1), before[k:])
                before = rs_list(q)
            else:
                lagged(before[k:], rs_list(q), RS_LAG)
                before = []
    run(before)
    for cond, make in pending:
        when(cond, lambda make=make: make().wait_send())


def local(shape, tokens, routes, gate_code, w_gate, w_up, w_down):
    Z, Y, C, ag_cut, rs_cut = shape
    n = Z * Y * C
    rows, D = tokens.shape
    F = w_gate.shape[2]
    Q = rows // ROWS
    wide = D + PAD
    ag_parts = tuple((a, b, m) for a, b, m in ((0, ag_cut, "y"), (ag_cut, D // 2, "z"), (D // 2, wide, "z")) if b > a)
    rs_parts = tuple((a, b, m) for a, b, m in ((0, rs_cut, "y"), (rs_cut, D, "z")) if b > a)
    NA, NR, ZY = len(ag_parts), len(rs_parts), Z * Y
    plan = (Z, Y, C, Q, D, ag_parts, rs_parts)
    bf = jnp.bfloat16
    dma = pltpu.SemaphoreType.DMA
    vmem = pl.BlockSpec(memory_space=pltpu.VMEM)
    hbm = pl.BlockSpec(memory_space=pl.ANY)
    z_rows = Q * ZY * ROWS
    return pl.pallas_call(
        functools.partial(kernel, plan),
        out_shape=jax.ShapeDtypeStruct((rows, D), bf),
        in_specs=[vmem, vmem, vmem, hbm, hbm, hbm],
        out_specs=vmem,
        scratch_shapes=[
            pltpu.VMEM((Q * n * ROWS, wide), bf),
            pltpu.VMEM((Q * n * ROWS, D), bf),
            pltpu.VMEM((n * ROWS, F), bf),
            pltpu.VMEM((z_rows, D), bf),
            pltpu.VMEM((Q * Z * ROWS, D), bf),
            pltpu.VMEM((z_rows, D), bf),
            pltpu.VMEM((z_rows, D), bf),
            pltpu.VMEM((D, F), bf),
            pltpu.VMEM((D, F), bf),
            pltpu.VMEM((F, D), bf),
            dma((Q, NA, n)), dma((Q, NA, 4, ZY)),
            dma((Q, NR)), dma((Q, NR)),
            dma((Q, NR, Z)), dma((Q, NR, Z)),
            dma((Q, NR, ZY)), dma((Q, NR, ZY)),
            dma((Q, NR, ZY)), dma((Q, NR, ZY)),
            dma((3,)),
        ],
        compiler_params=pltpu.CompilerParams(
            collective_id=0, has_side_effects=True, vmem_limit_bytes=60 * 1024 * 1024),
    )(tokens, routes.T, gate_code.T, w_gate[0], w_up[0], w_down[0])


def solution(mesh):
    n = mesh.shape["hst"]
    C = 2
    Y = 2 if n <= 16 else 1
    shape = (n // (C * Y), Y, C, AG_CUT if Y > 1 else 0, RS_CUT if Y > 1 else 0)
    rows = P(("group", "hst"), None)
    whole = P("hst", None, None)
    return jax.shard_map(functools.partial(local, shape), mesh=mesh,
                         in_specs=(rows, rows, rows, whole, whole, whole), out_specs=rows, check_vma=False)


AG_CUT = 0
RS_CUT = 512
AG_LAG = 3
RS_EARLY = 5
RS_LAG = 1
```
